768 devices in a mesh: dp: 12 (over z), et: 64 (over y, x, core).
Axes of the slice: x: 4, y: 8, z: 12, core: 2. Of those that a mesh axis runs over, the one named last changes fastest.
Arguments:
- hidden_t: bfloat16 [10752, 1536], P('et', 'dp'), may hold values from -6 to 6
- weights: bfloat16 [2, 10752, 6144], P(None, 'et'), may hold values from -0.15625 to 0.15625
- grad_out_t: bfloat16 [6144, 1536], P('et', 'dp'), may hold values from -1.1953125 to 1.1953125
- counts: int32 [12, 2], P('dp'), may hold values from 1 to 96, 128 in all within a row
- row_order: int32 [12, 128], P('dp'), may hold values from 0 to 127, each once within a row
Outputs:
- outputs_t: bfloat16 [6144, 1536], P('et', 'dp')
- grad_hidden_t: bfloat16 [10752, 1536], P('et', 'dp')
- grad_weights: bfloat16 [2, 10752, 6144], P(None, 'et', 'dp')
The draws below stay inside these ranges and needn't reach their ends.
Inputs may be any that keep to these rules, and one draw needn't show every extreme that they name: Each group's counts sum to 128, and no count exceeds 3 * 32. Each group's row_order is a permutation of its 128 rows.
All inputs are finite; a program needn't handle non-finite values.
Results may differ from the reference program's by a relative error of at most 0.02.
Values may be sent and summed in bfloat16 or wider, within the bound.
A program may use at most 32 MiB of HBM per device.

```python
import math
import jax
import jax.numpy as jnp
import numpy as np
from jax import lax

D = 6144
FF = 10752
E_WIN = 2
ROWS = 128
GROUPS = 12
N_DP = 12


def strengthened(entries, own_key, source, target, blocks, factor):
    def block_of(dim):
        return (jnp.arange(entries.shape[dim]) // (entries.shape[dim] // blocks)).reshape((-1,) + (1,) * (entries.ndim - 1 - dim))

    first = jax.random.permutation(own_key, blocks)[block_of(target)]
    other_side = (block_of(target) + blocks // 2) % blocks
    return jnp.where((block_of(source) == first) | (block_of(source) == other_side), factor * entries, entries)


def shard_levels(key, dims, cuts, low, largest):
    gain = 1.0
    for dim, blocks in cuts:
        heights = jax.random.uniform(jax.random.fold_in(jax.random.fold_in(key, 6), dim), (blocks,), jnp.float32, low / len(cuts), largest / len(cuts))
        gain = gain * jnp.repeat(jnp.exp(heights), dims[dim] // blocks).reshape((-1,) + (1,) * (len(dims) - 1 - dim))
    return gain


def split_up(count, total, most, skew):
    loads = [(1 << 20) // math.isqrt(rank ** skew) + 1 for rank in range(2, count + 1)]
    rest, holding = total - most - (count - 1), [1] * (count - 1)
    while rest > 0:
        candidates = [i for i in range(count - 1) if holding[i] < most]
        pool, remaining = sum([loads[i] for i in candidates]), rest
        for i in candidates:
            more = min(most - holding[i], max(1, remaining * loads[i] // pool), rest)
            holding[i] = holding[i] + more
            rest = rest - more
    return np.array([most] + holding)


def uneven_parts(stream_key, count, total, bound, skew):
    if count == 2:
        one = jax.random.randint(stream_key, (), max(1, total - bound), min(bound, total - 1) + 1)
        return jnp.stack([one, total - one])
    tallies = jnp.asarray(split_up(count, total, bound, skew), jnp.int32)
    pairs = (count - 1) // 2
    source_of, receiver = tallies[1:1 + 2 * pairs:2], tallies[2:2 + 2 * pairs:2]
    slack = jnp.minimum(source_of - 1, bound - receiver)
    shifted = jax.random.randint(jax.random.fold_in(stream_key, 1), (pairs,), 0, 1 << 20) % (slack + 1)
    tallies = tallies.at[1:1 + 2 * pairs:2].set(source_of - shifted).at[2:2 + 2 * pairs:2].set(receiver + shifted)
    return tallies[jax.random.permutation(jax.random.fold_in(stream_key, 2), count)]


def centred(rng, dims, scale, limit, cuts=(), held_as=jnp.bfloat16):
    values = jax.random.normal(rng, dims, jnp.float32) * scale
    if len(cuts) > 0:
        values = shard_levels(rng, dims, cuts, -0.22, 0.18) * values
    return jnp.clip(values, min=-limit, max=limit).astype(held_as)


def noise_with(key, extent, deviation, bound, split, heavy, kind=jnp.bfloat16):
    values = deviation * jax.random.normal(key, extent, jnp.float32)
    if split:
        values = values * shard_levels(key, extent, split, -0.22, 0.18)
    return jnp.clip(strengthened(values, jax.random.fold_in(key, 3), *heavy), -bound, bound).astype(kind)


def setup_inputs(seed: int = 0) -> dict:
    keys = jax.random.split(jax.random.key(seed), 6)
    return {
        "hidden_t": centred(keys[0], (FF, GROUPS * ROWS), 1.0, 6.0, ((0, 64), (1, 12))),
        "weights": noise_with(keys[1], (E_WIN, FF, D), FF ** -0.5, 0.15625, ((1, 64),), (1, 2, 64, 4.0)),
        "grad_out_t": centred(keys[2], (D, GROUPS * ROWS), 0.2, 1.1953125, ((0, 64), (1, 12))),
        "counts": jax.vmap(lambda own: uneven_parts(own, E_WIN, ROWS, 3 * ROWS // 4, 0))(jax.random.split(keys[3], GROUPS)).reshape((GROUPS, E_WIN)).astype(jnp.int32),
        "row_order": jax.vmap(lambda own: jax.random.permutation(own, ROWS))(jax.random.split(keys[4], GROUPS)).reshape((GROUPS, ROWS)).astype(jnp.int32),
    }


def routing(counts_row, order_row):
    positions = jnp.arange(order_row.shape[0], dtype=jnp.int32)
    bounds = jnp.cumsum(counts_row)[:-1]
    sorted_expert = jnp.sum((positions[:, None] >= bounds[None, :]).astype(jnp.int32), axis=1).astype(jnp.int32)
    return jnp.zeros((order_row.shape[0],), jnp.int32).at[order_row].set(sorted_expert)


def reference(hidden_t, weights, grad_out_t, counts, row_order):
    routed = jax.vmap(routing)(counts, row_order).reshape(-1)
    experts = weights.shape[0]
    outputs = jnp.zeros((weights.shape[2], hidden_t.shape[1]), jnp.float32)
    grad_hidden = jnp.zeros((weights.shape[1], hidden_t.shape[1]), jnp.float32)
    for expert in range(experts):
        picked = (routed == expert)[None, :]
        part = lax.dot_general(weights[expert], hidden_t, (((0,), (0,)), ((), ())), preferred_element_type=jnp.float32)
        outputs = outputs + jnp.where(picked, part, 0.0)
        back = jnp.dot(weights[expert], grad_out_t, preferred_element_type=jnp.float32)
        grad_hidden = grad_hidden + jnp.where(picked, back, 0.0)
    totals = [jnp.zeros((weights.shape[1], weights.shape[2]), jnp.float32) for expert in range(experts)]
    zero = jnp.zeros((), jnp.bfloat16)
    for group in range(N_DP):
        hidden_rows = hidden_t[:, group * ROWS:(group + 1) * ROWS]
        grad_rows = grad_out_t[:, group * ROWS:(group + 1) * ROWS]
        group_routes = routed[group * ROWS:(group + 1) * ROWS]
        for expert in range(experts):
            masked = jnp.where((group_routes == expert)[None, :], hidden_rows, zero)
            part = lax.dot_general(masked, grad_rows, (((1,), (1,)), ((), ())), preferred_element_type=jnp.float32)
            rounded = lax.optimization_barrier(part.astype(jnp.bfloat16)).astype(jnp.float32)
            totals[expert] = totals[expert] + rounded
    grad_weights = jnp.stack(totals).astype(jnp.bfloat16)
    return outputs.astype(jnp.bfloat16), grad_hidden.astype(jnp.bfloat16), grad_weights
```

```python
import jax
import jax.numpy as jnp
from jax import lax
from jax.experimental import pallas as pl
from jax.experimental.pallas import tpu as pltpu
from jax.sharding import PartitionSpec as P

MESH = pl.DeviceIdType.MESH
NY, NX, NZ = 8, 4, 12
BF16, F32 = jnp.bfloat16, jnp.float32


def dot(a, b, ca, cb):
    return lax.dot_general(a, b, (((ca,), (cb,)), ((), ())), preferred_element_type=F32)


def kernel(
    h_ref, w_hbm, g_ref, counts_ref, order_ref, out_ref, gh_ref, gw_ref,
    w_v, full, gath, hbuf, mbuf, hm, part, sibs, sibr, xs, xr, ys, yr,
    wsem, p_s, p_r, hz_s, hz_r, mz_s, mz_r,
    a1y_s, a1y_r, a1x_s, a1x_r, a1c_s, a1c_r,
    a2y_s, a2y_r, a2x_s, a2x_r, a2c_s, a2c_r,
    rc_s, rc_r, rx_s, rx_r, ry_s, ry_r,
):
    z = lax.axis_index("dp")
    et = lax.axis_index("et")
    y, x, c = et // 8, (et // 2) % 4, et % 2
    kq, ks = z // 3, z % 3

    def dev(yy, xx, cc):
        return (z, (yy * 4 + xx) * 2 + cc)

    def rem(a, n):
        return lax.rem(a + n, n)

    def ypeer(d):
        return dev(rem(y + d, NY), x, c)

    def xpeer(e):
        return dev(y, rem(x + e, NX), c)

    def zpeer(d):
        return (rem(z + d, NZ), et)

    sibling = dev(y, x, 1 - c)

    def remote(src, dst, ss, rs, peer):
        return pltpu.make_async_remote_copy(
            src_ref=src, dst_ref=dst, send_sem=ss, recv_sem=rs, device_id=peer, device_id_type=MESH
        )

    def unit_dest(t):
        u = et * 3 + t
        return u // 16, (u % 16) * 4 + kq

    my_w, my_kq = et // 4, et % 4
    my_u = z * 16 + my_w
    src_et, src_t = my_u // 3, my_u % 3

    def unit_source(s):
        return my_kq * 3 + s, src_et

    def far(n):
        return rem(y + 4 + (1 - 2 * (n % 2)) * ((n + 1) // 2), NY)

    def w_copy(n):
        yy = far(n)
        cols = pl.ds(pl.multiple_of(yy * 768, 768), 768)
        return pltpu.make_async_copy(w_hbm.at[:, :, cols], w_v.at[yy], wsem.at[n])

    for n in range(8):
        w_copy(n).start()

    bar = pltpu.get_barrier_semaphore()

    def greet(peer):
        pl.semaphore_signal(bar, inc=1, device_id=peer, device_id_type=MESH)

    for d in range(1, NY):
        greet(ypeer(d))
    for e in range(1, NX):
        greet(xpeer(e))
    greet(sibling)
    for d in range(1, NZ):
        greet(zpeer(d))

    def is_self(peer):
        return jnp.logical_and(peer[0] == z, peer[1] == et)

    greeted = 7 + 3 + 1 + 11
    for t in range(3):
        for peer in (unit_dest(t), unit_source(t)):
            own = is_self(peer)

            greeted = greeted + jnp.where(own, 0, 1)

            @pl.when(jnp.logical_not(own))
            def _():
                greet(peer)

    order = jnp.broadcast_to(order_ref[...].astype(F32), (128, 128)).T
    lane = lax.broadcasted_iota(jnp.int32, (128, 128), 1).astype(F32)
    pos = lax.broadcasted_iota(jnp.int32, (128, 128), 0)
    expert = (pos >= counts_ref[0, 0]).astype(F32)
    routed = jnp.sum(jnp.where(order == lane, expert, 0.0), axis=0, keepdims=True)
    mbuf[z] = jnp.broadcast_to(routed, (16, 128)).astype(BF16)
    h = h_ref[...]
    hbuf[z] = h
    for k in range(2):
        hm[k] = jnp.where(routed == float(k), h.astype(F32), 0.0).astype(BF16)
    full[y, x, c] = g_ref[...]

    pl.semaphore_wait(bar, greeted)

    def p_copy(t):
        i, j = unit_dest(t)
        w = (et * 3 + t) % 16
        return remote(
            g_ref.at[pl.ds(32 * t, 32)],
            gath.at[kq // 2, kq % 2, ks, w // 2, w % 2],
            p_s.at[t], p_r.at[ks], (i, j),
        )

    for t in range(3):
        peer = unit_dest(t)
        own = is_self(peer)

        @pl.when(jnp.logical_not(own))
        def _():
            p_copy(t).start()

        @pl.when(own)
        def _():
            w = (et * 3 + t) % 16
            gath[kq // 2, kq % 2, ks, w // 2, w % 2] = g_ref[pl.ds(32 * t, 32), :]

    def near(m):
        return ((m + 1) // 2) * (1 - 2 * ((m + 1) % 2))

    def a1y(d):
        return remote(g_ref, full.at[y, x, c], a1y_s.at[d], a1y_r.at[d], ypeer(d))

    def a1y_recv(m):
        d = rem(near(m), NY)
        yy = rem(y - d, NY)
        remote(g_ref, full.at[yy, x, c], a1y_s.at[d], a1y_r.at[d], ypeer(d)).wait_recv()

    def a1x(m, e):
        yy = rem(y - near(m), NY)
        i = m * 4 + e
        return remote(full.at[yy, x, c], full.at[yy, x, c], a1x_s.at[i], a1x_r.at[i], xpeer(e))

    def a1x_recv(m, e):
        yy = rem(y - near(m), NY)
        i = m * 4 + e
        blk = full.at[yy, rem(x - e, NX), c]
        remote(blk, blk, a1x_s.at[i], a1x_r.at[i], xpeer(e)).wait_recv()

    def a1c(m, cc):
        blk = full.at[rem(y - near(m), NY), :, cc]
        return remote(blk, blk, a1c_s.at[m], a1c_r.at[m], sibling)

    def gblk(yy, xx):
        return gath.at[xx % 2, c, :, yy, xx // 2]

    def a2y(d):
        return remote(gblk(y, x), gblk(y, x), a2y_s.at[d], a2y_r.at[d], ypeer(d))

    def a2y_recv(m):
        d = rem(near(m), NY)
        blk = gblk(rem(y - d, NY), x)
        remote(blk, blk, a2y_s.at[d], a2y_r.at[d], ypeer(d)).wait_recv()

    def a2x(m, e):
        blk = gblk(rem(y - near(m), NY), x)
        i = m * 4 + e
        return remote(blk, blk, a2x_s.at[i], a2x_r.at[i], xpeer(e))

    def a2x_recv(m, e):
        blk = gblk(rem(y - near(m), NY), rem(x - e, NX))
        i = m * 4 + e
        remote(blk, blk, a2x_s.at[i], a2x_r.at[i], xpeer(e)).wait_recv()

    def a2c(m, cc):
        blk = gath.at[:, cc, :, rem(y - near(m), NY)]
        return remote(blk, blk, a2c_s.at[m], a2c_r.at[m], sibling)

    def hz(d):
        return remote(h_ref, hbuf.at[z], hz_s.at[d], hz_r.at[d], zpeer(d))

    def hz_recv(d):
        remote(h_ref, hbuf.at[rem(z - d, NZ)], hz_s.at[d], hz_r.at[d], zpeer(d)).wait_recv()

    def mz(d):
        return remote(mbuf.at[z], mbuf.at[z], mz_s.at[d], mz_r.at[d], zpeer(d))

    def mz_recv(d):
        blk = mbuf.at[rem(z - d, NZ)]
        remote(blk, blk, mz_s.at[d], mz_r.at[d], zpeer(d)).wait_recv()

    for d in (4, 3, 5, 2, 6, 1, 7):
        a1y(d).start()
    for d in range(1, NZ):
        hz(d).start()
        mz(d).start()

    def rc(n):
        yy = far(n)
        return remote(sibs.at[yy], sibr.at[yy], rc_s.at[n], rc_r.at[n], sibling)

    def rx(n, e):
        yy = far(n)
        i = n * 4 + e
        return remote(xs.at[yy, rem(x + e, NX)], xr.at[yy, e], rx_s.at[i], rx_r.at[i], xpeer(e))

    def ry(n):
        yy = far(n)
        d = rem(yy - y, NY)
        return remote(ys.at[yy], yr.at[d], ry_s.at[d], ry_r.at[d], dev(yy, x, c))

    def step(n, carry):
        @pl.when(n < 8)
        def _():
            w_copy(n).wait()
            yy = far(n)
            p = dot(w_v[yy, 0], hm[0], 0, 0) + dot(w_v[yy, 1], hm[1], 0, 0)
            part[yy] = p.reshape(4, 2, 96, 128)
            sibs[yy] = part[yy, :, 1 - c].astype(BF16)
            rc(n).start()

        @pl.when(jnp.logical_and(n >= 1, n < 9))
        def _():
            m = n - 1
            yy = far(m)
            rc(m).wait_recv()
            total = part[yy, :, c] + sibr[yy].astype(F32)
            part[yy, :, c] = total
            xs[yy] = total.astype(BF16)
            for e in range(1, NX):
                rx(m, e).start()

        @pl.when(jnp.logical_and(n >= 2, n < 10))
        def _():
            m = n - 2
            yy = far(m)
            total = part[yy, x, c]
            for e in range(1, NX):
                rx(m, e).wait_recv()
                total = total + xr[yy, e].astype(F32)

            @pl.when(m < 7)
            def _():
                ys[yy] = total.astype(BF16)
                ry(m).start()

            @pl.when(m == 7)
            def _():
                part[yy, x, c] = total

        @pl.when(n >= 2)
        def _():
            m = n - 2

            @pl.when(m > 0)
            def _():
                a1y_recv(m)

            for e in range(1, NX):
                a1x(m, e).start()

        @pl.when(n == 6)
        def _():
            for s in range(3):
                own = is_self(unit_source(s))

                @pl.when(jnp.logical_not(own))
                def _():
                    blk = gath.at[my_kq // 2, my_kq % 2, s, my_w // 2, my_w % 2]
                    remote(blk, blk, p_s.at[0], p_r.at[s], sibling).wait_recv()

            for d in (4, 3, 5, 2, 6, 1, 7):
                a2y(d).start()

        return carry

    lax.fori_loop(0, 10, step, 0)

    def step2(m, carry):
        @pl.when(m > 0)
        def _():
            a2y_recv(m)

        for e in range(1, NX):
            a2x(m, e).start()
        for e in range(1, NX):
            a1x_recv(m, e)
        a1c(m, c).start()
        return carry

    lax.fori_loop(0, 8, step2, 0)

    total = part[y, x, c]
    for d in range(1, NY):
        remote(ys.at[y], yr.at[d], ry_s.at[d], ry_r.at[d], ypeer(d)).wait_recv()
        total = total + yr[d].astype(F32)
    out_ref[...] = total.astype(BF16)

    def step3(m, acc):
        a1c(m, 1 - c).wait_recv()
        yy = rem(y - near(m), NY)
        g = full[yy].reshape(768, 128)
        acc = tuple(acc[k] + dot(w_v[yy, k], g, 1, 0) for k in range(2))
        for e in range(1, NX):
            a2x_recv(m, e)
        a2c(m, c).start()
        return acc

    zero = jnp.zeros((168, 128), F32)
    back = lax.fori_loop(0, 8, step3, (zero, zero))
    gh_ref[...] = jnp.where(routed == 0.0, back[0], back[1]).astype(BF16)

    for d in range(1, NZ):
        hz_recv(d)
        mz_recv(d)
    for m in range(8):
        a2c(m, 1 - c).wait_recv()
    for k in range(2):
        hs, gs = [], []
        for i in range(12):
            mask = mbuf[i].astype(F32)[0:1]
            hs.append(jnp.where(mask == float(k), hbuf[i].astype(F32), 0.0).astype(BF16))
            q = i // 3
            gs.append(gath[q // 2, q % 2, i % 3].reshape(512, 128))
        gw_ref[k] = dot(jnp.concatenate(hs, axis=1), jnp.concatenate(gs, axis=1), 1, 1).astype(BF16)

    for t in range(3):

        @pl.when(jnp.logical_not(is_self(unit_dest(t))))
        def _():
            p_copy(t).wait_send()

    for d in range(1, NY):
        a1y(d).wait_send()
        a2y(d).wait_send()
        remote(ys.at[y], yr.at[d], ry_s.at[d], ry_r.at[d], ypeer(d)).wait_send()
    for d in range(1, NZ):
        hz(d).wait_send()
        mz(d).wait_send()

    def drain(m, carry):
        rc(m).wait_send()
        a1c(m, c).wait_send()
        a2c(m, c).wait_send()
        for e in range(1, NX):
            a1x(m, e).wait_send()
            a2x(m, e).wait_send()
            rx(m, e).wait_send()
        return carry

    lax.fori_loop(0, 8, drain, 0)


def shards(hidden_t, weights, grad_out_t, counts, row_order):
    vmem = pl.BlockSpec(memory_space=pltpu.VMEM)
    dma = pltpu.SemaphoreType.DMA
    blocks = (8, 4, 96, 128)
    return pl.pallas_call(
        kernel,
        out_shape=(
            jax.ShapeDtypeStruct((96, 128), BF16),
            jax.ShapeDtypeStruct((168, 128), BF16),
            jax.ShapeDtypeStruct((2, 168, 512), BF16),
        ),
        in_specs=[
            vmem,
            pl.BlockSpec(memory_space=pl.ANY),
            vmem,
            pl.BlockSpec(memory_space=pltpu.SMEM),
            vmem,
        ],
        out_specs=(vmem, vmem, vmem),
        scratch_shapes=[
            pltpu.VMEM((8, 2, 168, 768), BF16),
            pltpu.VMEM((8, 4, 2, 96, 128), BF16),
            pltpu.VMEM((2, 2, 3, 8, 2, 32, 128), BF16),
            pltpu.VMEM((12, 168, 128), BF16),
            pltpu.VMEM((12, 16, 128), BF16),
            pltpu.VMEM((2, 168, 128), BF16),
            pltpu.VMEM((8, 4, 2, 96, 128), F32),
            pltpu.VMEM(blocks, BF16),
            pltpu.VMEM(blocks, BF16),
            pltpu.VMEM(blocks, BF16),
            pltpu.VMEM(blocks, BF16),
            pltpu.VMEM((8, 96, 128), BF16),
            pltpu.VMEM((8, 96, 128), BF16),
            dma((8,)), dma((3,)), dma((3,)), dma((12,)), dma((12,)), dma((12,)), dma((12,)),
            dma((8,)), dma((8,)), dma((32,)), dma((32,)), dma((8,)), dma((8,)),
            dma((8,)), dma((8,)), dma((32,)), dma((32,)), dma((8,)), dma((8,)),
            dma((8,)), dma((8,)), dma((32,)), dma((32,)), dma((8,)), dma((8,)),
        ],
        compiler_params=pltpu.CompilerParams(
            collective_id=0, has_side_effects=True, vmem_limit_bytes=48 << 20
        ),
        name="moe_down",
    )(hidden_t, weights, grad_out_t, counts, row_order)


def solution(mesh):
    in_specs = (P("et", "dp"), P(None, "et", None), P("et", "dp"), P("dp", None), P("dp", None))
    out_specs = (P("et", "dp"), P("et", "dp"), P(None, "et", "dp"))
    return jax.shard_map(shards, mesh=mesh, in_specs=in_specs, out_specs=out_specs, check_vma=False)
```

```python
import jax
import jax.numpy as jnp
from jax import lax
from jax.experimental import pallas as pl
from jax.experimental.pallas import tpu as pltpu
from jax.sharding import PartitionSpec as P

MESH = pl.DeviceIdType.MESH
NY, NX, NZ = 8, 4, 12
BF16, F32 = jnp.bfloat16, jnp.float32


def dot(a, b, ca, cb):
    return lax.dot_general(a, b, (((ca,), (cb,)), ((), ())), preferred_element_type=F32)


def kernel(
    h_hbm, w_hbm, g_hbm, counts_hbm, order_hbm, out_ref, gh_ref, gw_ref,
    w_v, full, gath, hbuf, mbuf, hm, part, sibs, sibr, xs, xr, ys, yr, back, hcat, counts_v, order_v,
    wsem, in_sem, p_s, p_r, hz_s, hz_r, mz_s, mz_r,
    a1y_s, a1y_r, a1x_s, a1x_r, a1c_s, a1c_r,
    a2y_s, a2y_r, a2x_s, a2x_r, a2c_s, a2c_r,
    rc_s, rc_r, rx_s, rx_r, ry_s, ry_r,
):
    z = lax.axis_index("dp")
    et = lax.axis_index("et")
    y, x, c = et // 8, (et // 2) % 4, et % 2
    kq, ks = z // 3, z % 3

    def dev(yy, xx, cc):
        return (z, (yy * 4 + xx) * 2 + cc)

    def rem(a, n):
        return lax.rem(a + n, n)

    def ypeer(d):
        return dev(rem(y + d, NY), x, c)

    def xpeer(e):
        return dev(y, rem(x + e, NX), c)

    def zpeer(d):
        return (rem(z + d, NZ), et)

    sibling = dev(y, x, 1 - c)

    def remote(src, dst, ss, rs, peer):
        return pltpu.make_async_remote_copy(
            src_ref=src, dst_ref=dst, send_sem=ss, recv_sem=rs, device_id=peer, device_id_type=MESH
        )

    def unit_dest(t):
        u = et * 3 + t
        return u // 16, (u % 16) * 4 + kq

    my_w, my_kq = et // 4, et % 4
    src_et = (z * 16 + my_w) // 3

    def unit_source(s):
        return my_kq * 3 + s, src_et

    def far(n):
        return rem(y + 4 + (1 - 2 * (n % 2)) * ((n + 1) // 2), NY)

    def near(m):
        return ((m + 1) // 2) * (1 - 2 * ((m + 1) % 2))

    def side(m):
        return 1 - 2 * (m % 2)

    bar = pltpu.get_barrier_semaphore()

    def greet(peer):
        pl.semaphore_signal(bar, inc=1, device_id=peer, device_id_type=MESH)

    def is_self(peer):
        return jnp.logical_and(peer[0] == z, peer[1] == et)

    greeted = 7 + 2 + 1 + 6
    for t in range(3):
        for peer in (unit_dest(t), unit_source(t)):
            own = is_self(peer)
            greeted = greeted + jnp.where(own, 0, 1)

            @pl.when(jnp.logical_not(own))
            def _():
                greet(peer)

    for d in (4, 3, 5, 2, 6, 1, 7):
        greet(ypeer(d))
    for d in (3, -3, 2, -2, 1, -1):
        greet(zpeer(d))
    for e in (1, -1):
        greet(xpeer(e))
    greet(sibling)

    inputs = [
        pltpu.make_async_copy(src, dst, in_sem.at[i])
        for i, (src, dst) in enumerate(
            [
                (order_hbm, order_v),
                (counts_hbm, counts_v),
                (h_hbm, hbuf.at[z]),
                (g_hbm, full.at[y, x, c]),
            ]
        )
    ]
    for copy in inputs:
        copy.start()

    def w_copy(n):
        yy = far(n)
        cols = pl.ds(pl.multiple_of(yy * 768, 768), 768)
        return pltpu.make_async_copy(w_hbm.at[:, :, cols], w_v.at[yy], wsem.at[n])

    for n in range(8):
        w_copy(n).start()
    for copy in inputs:
        copy.wait()

    order = jnp.broadcast_to(order_v[...].astype(F32), (128, 128)).T
    lane = lax.broadcasted_iota(jnp.int32, (128, 128), 1).astype(F32)
    pos = lax.broadcasted_iota(jnp.int32, (128, 128), 0)
    expert = (pos >= counts_v[0:1, 0:1]).astype(F32)
    routed = jnp.sum(jnp.where(order == lane, expert, 0.0), axis=0, keepdims=True)
    mbuf[z] = jnp.broadcast_to(routed, (16, 128)).astype(BF16)
    h = hbuf[z].astype(F32)
    for k in range(2):
        hm[k] = jnp.where(routed == float(k), h, 0.0).astype(BF16)
        back[k] = jnp.zeros((168, 128), F32)

    pl.semaphore_wait(bar, greeted)

    g_own = full.at[y, x, c]

    def p_copy(t):
        w = (et * 3 + t) % 16
        return remote(
            full.at[y, x, c, pl.ds(32 * t, 32)],
            gath.at[kq // 2, kq % 2, ks, w // 2, w % 2],
            p_s.at[t], p_r.at[ks], unit_dest(t),
        )

    for t in range(3):
        own = is_self(unit_dest(t))

        @pl.when(jnp.logical_not(own))
        def _():
            p_copy(t).start()

        @pl.when(own)
        def _():
            w = (et * 3 + t) % 16
            gath[kq // 2, kq % 2, ks, w // 2, w % 2] = full[y, x, c, pl.ds(32 * t, 32), :]

    class Gather:
        def __init__(self, block, pair, sems):
            self.block, self.pair = block, pair
            self.ys, self.yr, self.xs, self.xr, self.cs, self.cr = sems

        def at(self, m, e):
            return self.block(rem(y - near(m), NY), rem(x + e, NX))

        def y_send(self, d):
            blk = self.block(y, x)
            return remote(blk, blk, self.ys.at[d], self.yr.at[d], ypeer(d))

        def y_recv(self, m):
            d = rem(near(m), NY)
            blk = self.at(m, 0)
            remote(blk, blk, self.ys.at[d], self.yr.at[d], ypeer(d)).wait_recv()

        def x_copy(self, m, e, i, to):
            blk = self.at(m, e)
            return remote(blk, blk, self.xs.at[m * 4 + i], self.xr.at[m * 4 + i], xpeer(to))

        def forward(self, m):
            @pl.when(m > 0)
            def _():
                self.y_recv(m)

            self.x_copy(m, 0, 0, 1).start()
            self.x_copy(m, 0, 1, -1).start()

        def relay(self, m):
            s = side(m)
            self.x_copy(m, -s, m % 2, s).wait_recv()
            self.x_copy(m, -s, 2, s).start()

        def finish(self, m):
            s = side(m)
            self.x_copy(m, s, 1 - m % 2, s).wait_recv()
            self.x_copy(m, 2, 2, s).wait_recv()
            self.c_copy(m, c).start()

        def c_copy(self, m, cc):
            blk = self.pair(rem(y - near(m), NY), cc)
            return remote(blk, blk, self.cs.at[m], self.cr.at[m], sibling)

        def drain(self, m):
            s = side(m)
            self.x_copy(m, 0, 0, 1).wait_send()
            self.x_copy(m, 0, 1, -1).wait_send()
            self.x_copy(m, -s, 2, s).wait_send()
            self.c_copy(m, c).wait_send()

    rows = Gather(
        lambda yy, xx: full.at[yy, xx, c],
        lambda yy, cc: full.at[yy, :, cc],
        (a1y_s, a1y_r, a1x_s, a1x_r, a1c_s, a1c_r),
    )
    plane = Gather(
        lambda yy, xx: gath.at[xx % 2, c, :, yy, xx // 2],
        lambda yy, cc: gath.at[:, cc, :, yy],
        (a2y_s, a2y_r, a2x_s, a2x_r, a2c_s, a2c_r),
    )

    for d in (4, 3, 5, 2, 6, 1, 7):
        rows.y_send(d).start()

    def hz(d, to, i):
        k = rem(z + d, NZ)
        return remote(hbuf.at[k], hbuf.at[k], hz_s.at[i], hz_r.at[i], zpeer(to))

    def mz(d, to, i):
        k = rem(z + d, NZ)
        return remote(mbuf.at[k], mbuf.at[k], mz_s.at[i], mz_r.at[i], zpeer(to))

    direct = [(0, d, d % 12) for d in (3, -3, 2, -2, 1, -1)]
    relays = [(-3, d, d + 3) for d in (1, 2, 3)] + [(3, -d, 9 - d) for d in (1, 2)]

    def z_start(hops):
        for d, to, i in hops:
            hz(d, to, i).start()
            mz(d, to, i).start()

    def z_recv(i):
        hz(-i, 1, i).wait_recv()
        mz(-i, 1, i).wait_recv()

    z_start(direct)

    def rc(n):
        yy = far(n)
        return remote(sibs.at[yy], sibr.at[yy], rc_s.at[n], rc_r.at[n], sibling)

    def rx(n, i):
        yy, s = far(n), side(n)
        e, to = ((2, s), (-s, -s), (s, s))[i]
        j = n * 4 + i
        return remote(xs.at[yy, rem(x + e, NX)], xr.at[yy, i], rx_s.at[j], rx_r.at[j], xpeer(to))

    def ry(n):
        yy = far(n)
        d = rem(yy - y, NY)
        return remote(ys.at[yy], yr.at[d], ry_s.at[d], ry_r.at[d], dev(yy, x, c))

    def ryf(d):
        return remote(ys.at[y], yr.at[d], ry_s.at[d], ry_r.at[d], ypeer(d))

    def project(n):
        w_copy(n).wait()
        yy = far(n)
        p = dot(w_v[yy, 0], hm[0], 0, 0) + dot(w_v[yy, 1], hm[1], 0, 0)
        part[yy] = p.reshape(4, 2, 96, 128)
        sibs[yy] = part[yy, :, 1 - c].astype(BF16)
        rc(n).start()

    def chip_sum(n):
        yy = far(n)
        rc(n).wait_recv()
        total = part[yy, :, c] + sibr[yy].astype(F32)
        part[yy, :, c] = total
        xs[yy] = total.astype(BF16)
        rx(n, 0).start()
        rx(n, 1).start()

    def x_relay(n):
        yy = far(n)
        e = rem(x + side(n), NX)
        rx(n, 0).wait_recv()
        xs[yy, e] = (part[yy, e, c] + xr[yy, 0].astype(F32)).astype(BF16)
        rx(n, 2).start()

    def x_sum(n):
        yy = far(n)
        rx(n, 1).wait_recv()
        rx(n, 2).wait_recv()
        total = part[yy, x, c] + xr[yy, 1].astype(F32) + xr[yy, 2].astype(F32)

        @pl.when(n < 7)
        def _():
            ys[yy] = total.astype(BF16)
            ry(n).start()

        @pl.when(n == 7)
        def _():
            part[yy, x, c] = total

    def grad_hidden(m):
        rows.c_copy(m, 1 - c).wait_recv()
        yy = rem(y - near(m), NY)
        g = full[yy].reshape(768, 128)
        for k in range(2):
            back[k] += dot(w_v[yy, k], g, 1, 0)

    def plane_start(m):
        for s in range(3):

            @pl.when(jnp.logical_not(is_self(unit_source(s))))
            def _():
                blk = gath.at[my_kq // 2, my_kq % 2, s, my_w // 2, my_w % 2]
                remote(blk, blk, p_s.at[0], p_r.at[s], sibling).wait_recv()

        for d in (4, 3, 5, 2, 6, 1, 7):
            plane.y_send(d).start()

    def z_relay(m):
        z_recv(3)
        z_recv(9)
        z_start(relays)

    stages = [
        (0, 8, project),
        (1, 8, chip_sum),
        (2, 8, rows.forward),
        (3, 8, x_relay),
        (4, 8, rows.relay),
        (5, 8, x_sum),
        (6, 8, rows.finish),
        (6, 1, plane_start),
        (7, 1, z_relay),
        (8, 8, plane.forward),
        (10, 8, plane.relay),
        (12, 8, plane.finish),
        (10, 8, grad_hidden),
    ]

    def step(n, carry):
        for first, count, stage in stages:

            @pl.when(jnp.logical_and(n >= first, n < first + count))
            def _():
                stage(n - first)

        return carry

    lax.fori_loop(0, max(first + count for first, count, _ in stages), step, 0)

    gh_ref[...] = jnp.where(routed == 0.0, back[0], back[1]).astype(BF16)

    total = part[y, x, c]
    for d in range(1, NY):
        ryf(d).wait_recv()
        total = total + yr[d].astype(F32)
    out_ref[...] = total.astype(BF16)

    for i in (1, 2, 10, 11, 4, 5, 6, 7, 8):
        z_recv(i)
    for i in range(12):
        mask = mbuf[i].astype(F32)[0:1]
        hi = hbuf[i].astype(F32)
        for k in range(2):
            hcat[k, :, 128 * i : 128 * i + 128] = jnp.where(mask == float(k), hi, 0.0).astype(BF16)
    for m in range(8):
        plane.c_copy(m, 1 - c).wait_recv()
    gs = [gath[i // 6, (i // 3) % 2, i % 3].reshape(512, 128) for i in range(12)]
    gs = jnp.concatenate(gs, axis=1)
    for k in range(2):
        gw_ref[k] = dot(hcat[k], gs, 1, 1).astype(BF16)

    for t in range(3):

        @pl.when(jnp.logical_not(is_self(unit_dest(t))))
        def _():
            p_copy(t).wait_send()

    for d in range(1, NY):
        rows.y_send(d).wait_send()
        plane.y_send(d).wait_send()
        ryf(d).wait_send()
    for d, to, i in direct + relays:
        hz(d, to, i).wait_send()
        mz(d, to, i).wait_send()

    def drain(m, carry):
        rc(m).wait_send()
        rows.drain(m)
        plane.drain(m)
        for i in range(3):
            rx(m, i).wait_send()
        return carry

    lax.fori_loop(0, 8, drain, 0)


def shards(hidden_t, weights, grad_out_t, counts, row_order):
    vmem = pl.BlockSpec(memory_space=pltpu.VMEM)
    dma = pltpu.SemaphoreType.DMA
    blocks = (8, 4, 96, 128)
    return pl.pallas_call(
        kernel,
        out_shape=(
            jax.ShapeDtypeStruct((96, 128), BF16),
            jax.ShapeDtypeStruct((168, 128), BF16),
            jax.ShapeDtypeStruct((2, 168, 512), BF16),
        ),
        in_specs=[pl.BlockSpec(memory_space=pl.ANY)] * 5,
        out_specs=(vmem, vmem, vmem),
        scratch_shapes=[
            pltpu.VMEM((8, 2, 168, 768), BF16),
            pltpu.VMEM((8, 4, 2, 96, 128), BF16),
            pltpu.VMEM((2, 2, 3, 8, 2, 32, 128), BF16),
            pltpu.VMEM((12, 168, 128), BF16),
            pltpu.VMEM((12, 16, 128), BF16),
            pltpu.VMEM((2, 168, 128), BF16),
            pltpu.VMEM((8, 4, 2, 96, 128), F32),
            pltpu.VMEM(blocks, BF16),
            pltpu.VMEM(blocks, BF16),
            pltpu.VMEM(blocks, BF16),
            pltpu.VMEM(blocks, BF16),
            pltpu.VMEM((8, 96, 128), BF16),
            pltpu.VMEM((8, 96, 128), BF16),
            pltpu.VMEM((2, 168, 128), F32),
            pltpu.VMEM((2, 168, 1536), BF16),
            pltpu.VMEM((1, 2), jnp.int32),
            pltpu.VMEM((1, 128), jnp.int32),
            dma((8,)), dma((4,)), dma((3,)), dma((3,)), dma((12,)), dma((12,)), dma((12,)), dma((12,)),
            dma((8,)), dma((8,)), dma((32,)), dma((32,)), dma((8,)), dma((8,)),
            dma((8,)), dma((8,)), dma((32,)), dma((32,)), dma((8,)), dma((8,)),
            dma((8,)), dma((8,)), dma((32,)), dma((32,)), dma((8,)), dma((8,)),
        ],
        compiler_params=pltpu.CompilerParams(
            collective_id=0, has_side_effects=True, vmem_limit_bytes=48 << 20
        ),
        name="moe_down",
    )(hidden_t, weights, grad_out_t, counts, row_order)


def solution(mesh):
    in_specs = (P("et", "dp"), P(None, "et", None), P("et", "dp"), P("dp", None), P("dp", None))
    out_specs = (P("et", "dp"), P("et", "dp"), P(None, "et", "dp"))
    return jax.shard_map(shards, mesh=mesh, in_specs=in_specs, out_specs=out_specs, check_vma=False)
```

```python
import jax
import jax.numpy as jnp
from jax import lax
from jax.experimental import pallas as pl
from jax.experimental.pallas import tpu as pltpu
from jax.sharding import PartitionSpec as P

MESH = pl.DeviceIdType.MESH
NY, NX, NZ = 8, 4, 12
BF16, F32 = jnp.bfloat16, jnp.float32


def dot(a, b, ca, cb):
    return lax.dot_general(a, b, (((ca,), (cb,)), ((), ())), preferred_element_type=F32)


def kernel(
    h_hbm, w_hbm, g_hbm, counts_hbm, order_hbm, out_ref, gh_ref, gw_ref,
    w_v, full, gath, hbuf, h_v, hm, part, sibs, sibr, xs, xr, ys, yr, back, hcat, gwt, counts_v, order_v,
    wsem, in_sem, p_s, p_r, hz_s, hz_r,
    a1y_s, a1y_r, a1x_s, a1x_r, a1c_s, a1c_r,
    a2y_s, a2y_r, a2x_s, a2x_r, a2c_s, a2c_r,
    rc_s, rc_r, rx_s, rx_r, ry_s, ry_r,
):
    z = lax.axis_index("dp")
    et = lax.axis_index("et")
    y, x, c = et // 8, (et // 2) % 4, et % 2

    def dev(yy, xx, cc):
        return (z, (yy * 4 + xx) * 2 + cc)

    def rem(a, n):
        return lax.rem(a + n, n)

    def ypeer(d):
        return dev(rem(y + d, NY), x, c)

    def xpeer(e):
        return dev(y, rem(x + e, NX), c)

    def zpeer(d):
        return (rem(z + d, NZ), et)

    sibling = dev(y, x, 1 - c)

    def remote(src, dst, ss, rs, peer):
        return pltpu.make_async_remote_copy(
            src_ref=src, dst_ref=dst, send_sem=ss, recv_sem=rs, device_id=peer, device_id_type=MESH
        )

    def corner(i):
        chip = i * 16 // 6
        return chip // 4, rem(chip % 4 - jnp.where(i % 3 == 0, 1, 0), NX)

    def groups_of(k, i):
        rel = rem(k - i, NZ) + 1
        return (rel // 3) % 4, rel % 3

    def group(i, q, s):
        return (i + 3 * q + s + 11) % NZ

    def place(i, w, q):
        yc, xc = corner(i)
        xo, b, cc = w // 8 * 2 + w // 2 % 2, w // 4 % 2, w % 2
        rank = jnp.where(q == 0, 3, jnp.where(q == 3, 2, 2 - q))
        yy = (yc + jnp.where(b == 1, 1 + rank, 8 - rank)) % NY
        return (yy * 4 + (xc + xo) % NX) * 2 + cc

    def row_of(i, yy):
        dy = rem(yy - corner(i)[0], NY)
        b = (dy + 3) % 8 // 4
        rank = jnp.where(b == 1, dy - 1, (8 - dy) % 8)
        return jnp.where(rank == 3, 0, jnp.where(rank == 2, 3, 2 - rank)), b

    def col_of(i, xx):
        return rem(xx - corner(i)[1], NX)

    def unit(t):
        u = et * 3 + t
        return u // 16, u % 16

    def unit_dest(t):
        i, w = unit(t)
        return i, place(i, w, groups_of(z, i)[0])

    def unit_slot(t):
        i, w = unit(t)
        q, s = groups_of(z, i)
        return gath.at[q, s, w // 8, w // 4 % 2, w // 2 % 2, w % 2], s

    my_q, my_b = row_of(z, y)
    my_xo = col_of(z, x)
    my_w = my_xo // 2 * 8 + my_b * 4 + my_xo % 2 * 2 + c

    def unit_source(s):
        return group(z, my_q, s), (z * 16 + my_w) // 3

    def far(n):
        return rem(y + 4 + (1 - 2 * (n % 2)) * ((n + 1) // 2), NY)

    def near(m):
        return ((m + 1) // 2) * (1 - 2 * ((m + 1) % 2))

    def side(m):
        return 1 - 2 * (m % 2)

    bar = pltpu.get_barrier_semaphore()

    def greet(peer):
        pl.semaphore_signal(bar, inc=1, device_id=peer, device_id_type=MESH)

    def is_self(peer):
        return jnp.logical_and(peer[0] == z, peer[1] == et)

    greeted = 7 + 2 + 1 + 6
    for t in range(3):
        for peer in (unit_dest(t), unit_source(t)):
            own = is_self(peer)
            greeted = greeted + jnp.where(own, 0, 1)

            @pl.when(jnp.logical_not(own))
            def _():
                greet(peer)

    for d in (4, 3, 5, 2, 6, 1, 7):
        greet(ypeer(d))
    for d in (3, -3, 2, -2, 1, -1):
        greet(zpeer(d))
    for e in (1, -1):
        greet(xpeer(e))
    greet(sibling)

    inputs = [
        pltpu.make_async_copy(src, dst, in_sem.at[i])
        for i, (src, dst) in enumerate(
            [
                (order_hbm, order_v),
                (counts_hbm, counts_v),
                (h_hbm, h_v),
                (g_hbm, full.at[y, x, c]),
            ]
        )
    ]
    for copy in inputs:
        copy.start()

    def w_copy(n):
        yy = far(n)
        cols = pl.ds(pl.multiple_of(yy * 768, 768), 768)
        return pltpu.make_async_copy(w_hbm.at[:, :, cols], w_v.at[yy], wsem.at[n])

    for n in range(8):
        w_copy(n).start()
    for copy in inputs:
        copy.wait()

    order = jnp.broadcast_to(order_v[...].astype(F32), (128, 128)).T
    lane = lax.broadcasted_iota(jnp.int32, (128, 128), 1).astype(F32)
    pos = lax.broadcasted_iota(jnp.int32, (128, 128), 0)
    expert = (pos >= counts_v[0:1, 0:1]).astype(F32)
    routed = jnp.sum(jnp.where(order == lane, expert, 0.0), axis=0, keepdims=True)
    h = h_v[...].astype(F32)
    hbuf[z] = jnp.concatenate(
        [h, jnp.zeros((8, 128), F32), jnp.broadcast_to(routed, (16, 128))], axis=0
    ).astype(BF16)
    for k in range(2):
        hm[k] = jnp.where(routed == float(k), h, 0.0).astype(BF16)
        back[k] = jnp.zeros((168, 128), F32)
        gwt[k] = jnp.zeros((2, 168, 256), F32)

    pl.semaphore_wait(bar, greeted)

    def p_copy(t):
        dst, s = unit_slot(t)
        src = full.at[y, x, c, pl.ds(32 * t, 32)]
        return remote(src, dst, p_s.at[t], p_r.at[s], unit_dest(t))

    for t in range(3):
        own = is_self(unit_dest(t))

        @pl.when(jnp.logical_not(own))
        def _():
            p_copy(t).start()

        @pl.when(own)
        def _():
            unit_slot(t)[0][...] = full[y, x, c, pl.ds(32 * t, 32), :]

    class Gather:
        def __init__(self, block, pair, relayed, sems):
            self.block, self.pair, self.relayed = block, pair, relayed
            self.ys, self.yr, self.xs, self.xr, self.cs, self.cr = sems

        def at(self, m, e):
            return self.block(rem(y - near(m), NY), rem(x + e, NX))

        def y_send(self, d):
            blk = self.block(y, x)
            return remote(blk, blk, self.ys.at[d], self.yr.at[d], ypeer(d))

        def y_recv(self, m):
            d = rem(near(m), NY)
            blk = self.at(m, 0)
            remote(blk, blk, self.ys.at[d], self.yr.at[d], ypeer(d)).wait_recv()

        def x_copy(self, m, e, i, to):
            blk = self.at(m, e)
            return remote(blk, blk, self.xs.at[m * 4 + i], self.xr.at[m * 4 + i], xpeer(to))

        def forward(self, m):
            @pl.when(m > 0)
            def _():
                self.y_recv(m)

            self.x_copy(m, 0, 0, 1).start()
            self.x_copy(m, 0, 1, -1).start()
            if not self.relayed:
                self.x_copy(m, 0, 2, 2).start()

        def relay(self, m):
            s = side(m)
            self.x_copy(m, -s, m % 2, s).wait_recv()
            self.x_copy(m, -s, 2, s).start()

        def finish(self, m):
            s = side(m)
            if self.relayed:
                self.x_copy(m, s, 1 - m % 2, s).wait_recv()
            else:
                self.x_copy(m, -1, 0, 1).wait_recv()
                self.x_copy(m, 1, 1, -1).wait_recv()
            self.x_copy(m, 2, 2, s).wait_recv()
            self.c_copy(m, c).start()

        def c_copy(self, m, cc):
            blk = self.pair(rem(y - near(m), NY), cc)
            return remote(blk, blk, self.cs.at[m], self.cr.at[m], sibling)

        def drain(self, m):
            s = side(m)
            self.x_copy(m, 0, 0, 1).wait_send()
            self.x_copy(m, 0, 1, -1).wait_send()
            if self.relayed:
                self.x_copy(m, -s, 2, s).wait_send()
            else:
                self.x_copy(m, 0, 2, 2).wait_send()
            self.c_copy(m, c).wait_send()

    rows = Gather(
        lambda yy, xx: full.at[yy, xx, c],
        lambda yy, cc: full.at[yy, :, cc],
        True,
        (a1y_s, a1y_r, a1x_s, a1x_r, a1c_s, a1c_r),
    )
    def plane_block(yy, xx):
        q, b = row_of(z, yy)
        xo = col_of(z, xx)
        return gath.at[q, :, xo // 2, b, xo % 2, c]

    def plane_pair(yy, cc):
        q, b = row_of(z, yy)
        return gath.at[q, :, :, b, :, cc]

    plane = Gather(
        plane_block,
        plane_pair,
        False,
        (a2y_s, a2y_r, a2x_s, a2x_r, a2c_s, a2c_r),
    )

    for d in (1, 7, 2, 6, 3, 5, 4):
        rows.y_send(d).start()

    def hz(d, to, i):
        k = rem(z + d, NZ)
        return remote(hbuf.at[k], hbuf.at[k], hz_s.at[i], hz_r.at[i], zpeer(to))

    direct = [(0, d, d % 12) for d in (3, -3, 2, -2, 1, -1)]
    relays = [(-3, d, d + 3) for d in (1, 2, 3)] + [(3, -d, 9 - d) for d in (1, 2)]

    def z_start(hops):
        for d, to, i in hops:
            hz(d, to, i).start()

    def z_recv(i):
        hz(-i, 1, i).wait_recv()

    z_start(direct)

    def rc(n):
        yy = far(n)
        return remote(sibs.at[yy], sibr.at[yy], rc_s.at[n], rc_r.at[n], sibling)

    def rx(n, i):
        yy, s = far(n), side(n)
        e, to = ((2, s), (-s, -s), (s, s))[i]
        j = n * 4 + i
        return remote(xs.at[yy, rem(x + e, NX)], xr.at[yy, i], rx_s.at[j], rx_r.at[j], xpeer(to))

    def ry(n):
        yy = far(n)
        d = rem(yy - y, NY)
        return remote(ys.at[yy], yr.at[d], ry_s.at[d], ry_r.at[d], dev(yy, x, c))

    def ryf(d):
        return remote(ys.at[y], yr.at[d], ry_s.at[d], ry_r.at[d], ypeer(d))

    def project(n):
        w_copy(n).wait()
        yy = far(n)
        p = dot(w_v[yy, 0], hm[0], 0, 0) + dot(w_v[yy, 1], hm[1], 0, 0)
        part[yy] = p.reshape(4, 2, 96, 128)
        sibs[yy] = part[yy, :, 1 - c].astype(BF16)
        rc(n).start()

    def chip_sum(n):
        yy = far(n)
        rc(n).wait_recv()
        total = part[yy, :, c] + sibr[yy].astype(F32)
        part[yy, :, c] = total
        xs[yy] = total.astype(BF16)
        rx(n, 0).start()
        rx(n, 1).start()

    def x_relay(n):
        yy = far(n)
        e = rem(x + side(n), NX)
        rx(n, 0).wait_recv()
        xs[yy, e] = (part[yy, e, c] + xr[yy, 0].astype(F32)).astype(BF16)
        rx(n, 2).start()

    def x_sum(n):
        yy = far(n)
        rx(n, 1).wait_recv()
        rx(n, 2).wait_recv()
        total = part[yy, x, c] + xr[yy, 1].astype(F32) + xr[yy, 2].astype(F32)

        @pl.when(n < 7)
        def _():
            ys[yy] = total.astype(BF16)
            ry(n).start()

        @pl.when(n == 7)
        def _():
            part[yy, x, c] = total

    def grad_hidden(m):
        rows.c_copy(m, 1 - c).wait_recv()
        yy = rem(y - near(m), NY)
        g = full[yy].reshape(768, 128)
        for k in range(2):
            back[k] += dot(w_v[yy, k], g, 1, 0)

    def plane_start(m):
        for s in range(3):

            @pl.when(jnp.logical_not(is_self(unit_source(s))))
            def _():
                blk = gath.at[my_q, s, my_xo // 2, my_b, my_xo % 2, c]
                remote(blk, blk, p_s.at[0], p_r.at[s], sibling).wait_recv()

        for d in (1, 7, 2, 6, 3, 5, 4):
            plane.y_send(d).start()

    def z_relay(m):
        z_recv(3)
        z_recv(9)
        z_start(relays)

    def z_finish(m):
        for i in (1, 2, 10, 11, 4, 5, 6, 7, 8):
            z_recv(i)
        for q in range(4):
            for s in range(3):
                block = hbuf[group(z, q, s)].astype(F32)
                mask = block[176:177]
                for k in range(2):
                    hcat[q, k, :, 128 * s : 128 * s + 128] = jnp.where(
                        mask == float(k), block[:168], 0.0
                    ).astype(BF16)

    def grad_weights(m):
        plane.c_copy(m, 1 - c).wait_recv()
        q, b = row_of(z, rem(y - near(m), NY))
        g = [gath[q, s, :, b].reshape(256, 128) for s in range(3)]
        g = jnp.concatenate(g, axis=1)
        for k in range(2):
            gwt[k, b] += dot(hcat[q, k], g, 1, 1)

    stages = [
        (0, 8, project),
        (1, 8, chip_sum),
        (2, 8, rows.forward),
        (3, 8, x_relay),
        (4, 8, rows.relay),
        (5, 8, x_sum),
        (4, 1, z_relay),
        (6, 1, plane_start),
        (6, 8, rows.finish),
        (8, 8, plane.forward),
        (8, 8, grad_hidden),
        (11, 1, z_finish),
        (11, 8, plane.finish),
        (12, 8, grad_weights),
    ]

    def step(n, carry):
        for first, count, stage in stages:

            @pl.when(jnp.logical_and(n >= first, n < first + count))
            def _():
                stage(n - first)

        return carry

    lax.fori_loop(0, max(first + count for first, count, _ in stages), step, 0)

    gh_ref[...] = jnp.where(routed == 0.0, back[0], back[1]).astype(BF16)

    total = part[y, x, c]
    for d in range(1, NY):
        ryf(d).wait_recv()
        total = total + yr[d].astype(F32)
    out_ref[...] = total.astype(BF16)

    for k in range(2):
        for b in range(2):
            for i in range(2):
                cols = slice(256 * i + 128 * b, 256 * i + 128 * b + 128)
                gw_ref[k, :, cols] = gwt[k, b, :, 128 * i : 128 * i + 128].astype(BF16)

    for t in range(3):

        @pl.when(jnp.logical_not(is_self(unit_dest(t))))
        def _():
            p_copy(t).wait_send()

    for d in range(1, NY):
        rows.y_send(d).wait_send()
        plane.y_send(d).wait_send()
        ryf(d).wait_send()
    for d, to, i in direct + relays:
        hz(d, to, i).wait_send()

    def drain(m, carry):
        rc(m).wait_send()
        rows.drain(m)
        plane.drain(m)
        for i in range(3):
            rx(m, i).wait_send()
        return carry

    lax.fori_loop(0, 8, drain, 0)


def shards(hidden_t, weights, grad_out_t, counts, row_order):
    vmem = pl.BlockSpec(memory_space=pltpu.VMEM)
    dma = pltpu.SemaphoreType.DMA
    blocks = (8, 4, 96, 128)
    return pl.pallas_call(
        kernel,
        out_shape=(
            jax.ShapeDtypeStruct((96, 128), BF16),
            jax.ShapeDtypeStruct((168, 128), BF16),
            jax.ShapeDtypeStruct((2, 168, 512), BF16),
        ),
        in_specs=[pl.BlockSpec(memory_space=pltpu.HBM)] * 5,
        out_specs=(vmem, vmem, vmem),
        scratch_shapes=[
            pltpu.VMEM((8, 2, 168, 768), BF16),
            pltpu.VMEM((8, 4, 2, 96, 128), BF16),
            pltpu.VMEM((4, 3, 2, 2, 2, 2, 32, 128), BF16),
            pltpu.VMEM((12, 192, 128), BF16),
            pltpu.VMEM((168, 128), BF16),
            pltpu.VMEM((2, 168, 128), BF16),
            pltpu.VMEM((8, 4, 2, 96, 128), F32),
            pltpu.VMEM(blocks, BF16),
            pltpu.VMEM(blocks, BF16),
            pltpu.VMEM(blocks, BF16),
            pltpu.VMEM(blocks, BF16),
            pltpu.VMEM((8, 96, 128), BF16),
            pltpu.VMEM((8, 96, 128), BF16),
            pltpu.VMEM((2, 168, 128), F32),
            pltpu.VMEM((4, 2, 168, 384), BF16),
            pltpu.VMEM((2, 2, 168, 256), F32),
            pltpu.VMEM((1, 2), jnp.int32),
            pltpu.VMEM((1, 128), jnp.int32),
            dma((8,)), dma((4,)), dma((3,)), dma((3,)), dma((12,)), dma((12,)),
            dma((8,)), dma((8,)), dma((32,)), dma((32,)), dma((8,)), dma((8,)),
            dma((8,)), dma((8,)), dma((32,)), dma((32,)), dma((8,)), dma((8,)),
            dma((8,)), dma((8,)), dma((32,)), dma((32,)), dma((8,)), dma((8,)),
        ],
        compiler_params=pltpu.CompilerParams(
            collective_id=0, has_side_effects=True, vmem_limit_bytes=60 << 20
        ),
        name="moe_down",
    )(hidden_t, weights, grad_out_t, counts, row_order)


def solution(mesh):
    in_specs = (P("et", "dp"), P(None, "et", None), P("et", "dp"), P("dp", None), P("dp", None))
    out_specs = (P("et", "dp"), P("et", "dp"), P(None, "et", "dp"))
    return jax.shard_map(shards, mesh=mesh, in_specs=in_specs, out_specs=out_specs, check_vma=False)
```

```python
import jax
import jax.numpy as jnp
from jax import lax
from jax.experimental import pallas as pl
from jax.experimental.pallas import tpu as pltpu
from jax.sharding import PartitionSpec as P

MESH = pl.DeviceIdType.MESH
NY, NX, NZ = 8, 4, 12
BF16, F32 = jnp.bfloat16, jnp.float32


def dot(a, b, ca, cb):
    return lax.dot_general(a, b, (((ca,), (cb,)), ((), ())), preferred_element_type=F32)


def kernel(
    h_hbm, w_hbm, g_hbm, counts_hbm, order_hbm, out_ref, gh_ref, gw_ref,
    w_v, full, gath, hbuf, h_v, hm, part, sibs, sibr, xs, xr, ys, yr, back, hcat, gwt, counts_v, order_v,
    wsem, in_sem, p_s, p_r, hz_s, hz_r,
    a1y_s, a1y_r, a1x_s, a1x_r, a1c_s, a1c_r,
    a2y_s, a2y_r, a2x_s, a2x_r, a2c_s, a2c_r,
    rc_s, rc_r, rx_s, rx_r, ry_s, ry_r,
):
    z = lax.axis_index("dp")
    et = lax.axis_index("et")
    y, x, c = et // 8, (et // 2) % 4, et % 2

    def dev(yy, xx, cc):
        return (z, (yy * 4 + xx) * 2 + cc)

    def rem(a, n):
        return lax.rem(a + n, n)

    def ypeer(d):
        return dev(rem(y + d, NY), x, c)

    def xpeer(e):
        return dev(y, rem(x + e, NX), c)

    def zpeer(d):
        return (rem(z + d, NZ), et)

    sibling = dev(y, x, 1 - c)

    def remote(src, dst, ss, rs, peer):
        return pltpu.make_async_remote_copy(
            src_ref=src, dst_ref=dst, send_sem=ss, recv_sem=rs, device_id=peer, device_id_type=MESH
        )

    def corner(i):
        chip = i * 16 // 6
        return chip // 4, rem(chip % 4 - jnp.where(i % 3 == 0, 1, 0), NX)

    def groups_of(k, i):
        rel = rem(k - i, NZ) + 1
        return (rel // 3) % 4, rel % 3

    def group(i, q, s):
        return (i + 3 * q + s + 11) % NZ

    def place(i, w, q):
        yc, xc = corner(i)
        xo, b, cc = w // 8 * 2 + w // 2 % 2, w // 4 % 2, w % 2
        rank = jnp.where(q == 0, 3, jnp.where(q == 3, 2, 2 - q))
        yy = (yc + jnp.where(b == 1, 1 + rank, 8 - rank)) % NY
        return (yy * 4 + (xc + xo) % NX) * 2 + cc

    def row_of(i, yy):
        dy = rem(yy - corner(i)[0], NY)
        b = (dy + 3) % 8 // 4
        rank = jnp.where(b == 1, dy - 1, (8 - dy) % 8)
        return jnp.where(rank == 3, 0, jnp.where(rank == 2, 3, 2 - rank)), b

    def col_of(i, xx):
        return rem(xx - corner(i)[1], NX)

    def unit(t):
        u = et * 3 + t
        return u // 16, u % 16

    def unit_dest(t):
        i, w = unit(t)
        return i, place(i, w, groups_of(z, i)[0])

    def unit_slot(t):
        i, w = unit(t)
        q, s = groups_of(z, i)
        return gath.at[q, s, w // 8, w // 4 % 2, w // 2 % 2, w % 2], s

    my_q, my_b = row_of(z, y)
    my_xo = col_of(z, x)
    my_w = my_xo // 2 * 8 + my_b * 4 + my_xo % 2 * 2 + c

    def unit_source(s):
        return group(z, my_q, s), (z * 16 + my_w) // 3

    def far(n):
        return rem(y + 4 + (1 - 2 * (n % 2)) * ((n + 1) // 2), NY)

    def near(m):
        return ((m + 1) // 2) * (1 - 2 * ((m + 1) % 2))

    def side(m):
        return 1 - 2 * (m % 2)

    inputs = [
        pltpu.make_async_copy(src, dst, in_sem.at[i])
        for i, (src, dst) in enumerate(
            [
                (order_hbm, order_v),
                (counts_hbm, counts_v),
                (h_hbm, h_v),
                (g_hbm, full.at[y, x, c]),
            ]
        )
    ]
    for copy in inputs[::-1]:
        copy.start()

    def w_copy(n):
        yy = far(n)
        cols = pl.ds(pl.multiple_of(yy * 768, 768), 768)
        return pltpu.make_async_copy(w_hbm.at[:, :, cols], w_v.at[yy], wsem.at[n])

    for n in range(8):
        w_copy(n).start()

    bar = pltpu.get_barrier_semaphore()

    def greet(peer):
        pl.semaphore_signal(bar, inc=1, device_id=peer, device_id_type=MESH)

    def is_self(peer):
        return jnp.logical_and(peer[0] == z, peer[1] == et)

    greeted = 7 + 3 + 1 + 6
    for t in range(3):
        for peer in (unit_dest(t), unit_source(t)):
            own = is_self(peer)
            greeted = greeted + jnp.where(own, 0, 1)

            @pl.when(jnp.logical_not(own))
            def _():
                greet(peer)

    for d in (4, 3, 5, 2, 6, 1, 7):
        greet(ypeer(d))
    for d in (3, -3, 2, -2, 1, -1):
        greet(zpeer(d))
    for e in (1, 2, 3):
        greet(xpeer(e))
    greet(sibling)

    def p_copy(t):
        dst, s = unit_slot(t)
        src = full.at[y, x, c, pl.ds(32 * t, 32)]
        return remote(src, dst, p_s.at[t], p_r.at[s], unit_dest(t))

    class Gather:
        def __init__(self, block, pair, sems):
            self.block, self.pair = block, pair
            self.ys, self.yr, self.xs, self.xr, self.cs, self.cr = sems

        def at(self, m, e):
            return self.block(rem(y - near(m), NY), rem(x + e, NX))

        def y_send(self, d):
            blk = self.block(y, x)
            return remote(blk, blk, self.ys.at[d], self.yr.at[d], ypeer(d))

        def y_recv(self, m):
            d = rem(near(m), NY)
            blk = self.at(m, 0)
            remote(blk, blk, self.ys.at[d], self.yr.at[d], ypeer(d)).wait_recv()

        def x_copy(self, m, e, i, to):
            blk = self.at(m, e)
            return remote(blk, blk, self.xs.at[m * 4 + i], self.xr.at[m * 4 + i], xpeer(to))

        def forward(self, m):
            @pl.when(m > 0)
            def _():
                self.y_recv(m)

            self.x_copy(m, 0, 0, 1).start()
            self.x_copy(m, 0, 1, -1).start()
            self.x_copy(m, 0, 2, 2).start()

        def finish(self, m):
            self.x_copy(m, -1, 0, 1).wait_recv()
            self.x_copy(m, 1, 1, -1).wait_recv()
            self.x_copy(m, 2, 2, 2).wait_recv()
            self.c_copy(m, c).start()

        def c_copy(self, m, cc):
            blk = self.pair(rem(y - near(m), NY), cc)
            return remote(blk, blk, self.cs.at[m], self.cr.at[m], sibling)

        def drain(self, m):
            self.x_copy(m, 0, 0, 1).wait_send()
            self.x_copy(m, 0, 1, -1).wait_send()
            self.x_copy(m, 0, 2, 2).wait_send()
            self.c_copy(m, c).wait_send()

    class Ring:
        def x_copy(self, e, e_from):
            blk = full.at[y, rem(x - e_from, NX), c]
            return remote(blk, blk, a1x_s.at[e], a1x_r.at[e], xpeer(e))

        def y_copy(self, way, s, g, shift):
            yy = rem(y - way * (s + shift), NY)
            blk = full.at[yy, pl.ds(2 * g, 2), c]
            i = (4 if way < 0 else 0) + s
            return remote(blk, blk, a1y_s.at[i, g], a1y_r.at[i, g], ypeer(way))

        def c_copy(self, m, cc):
            blk = full.at[rem(y - near(m), NY), :, cc]
            return remote(blk, blk, a1c_s.at[m], a1c_r.at[m], sibling)

        def hops(self, s):
            return [(w, g) for g in range(2) for w in (1, -1) if s < 3 or (w > 0) == (g == 0)]

        def start(self):
            for e in (1, 3, 2):
                self.x_copy(e, 0).start()

        def level(self, s):
            if s == 0:
                for e in (1, 3, 2):
                    self.x_copy(e, e).wait_recv()
            if s < 4:
                for w, g in self.hops(s):
                    if s > 0:
                        self.y_copy(w, s - 1, g, 1).wait_recv()
                    self.y_copy(w, s, g, 0).start()
                if s == 3:
                    for w, g in self.hops(0):
                        if (w, g) not in self.hops(3):
                            self.y_copy(w, 2, g, 1).wait_recv()
            else:
                for w, g in self.hops(3):
                    self.y_copy(w, 3, g, 1).wait_recv()
            for m in {0: (0,), 4: (7,)}.get(s, (2 * s - 1, 2 * s)):
                self.c_copy(m, c).start()

        def drain(self):
            for e in (1, 3, 2):
                self.x_copy(e, 0).wait_send()
            for s in range(4):
                for w, g in self.hops(s):
                    self.y_copy(w, s, g, 0).wait_send()
            for m in range(8):
                self.c_copy(m, c).wait_send()

    rows = Ring()
    def plane_block(yy, xx):
        q, b = row_of(z, yy)
        xo = col_of(z, xx)
        return gath.at[q, :, xo // 2, b, xo % 2, c]

    def plane_pair(yy, cc):
        q, b = row_of(z, yy)
        return gath.at[q, :, :, b, :, cc]

    plane = Gather(
        plane_block,
        plane_pair,
        (a2y_s, a2y_r, a2x_s, a2x_r, a2c_s, a2c_r),
    )


    def hz(d, to, i):
        k = rem(z + d, NZ)
        return remote(hbuf.at[k], hbuf.at[k], hz_s.at[i], hz_r.at[i], zpeer(to))

    direct = [(0, d, d % 12) for d in (3, -3, 2, -2, 1, -1)]
    relays = [(-3, d, d + 3) for d in (1, 2, 3)] + [(3, -d, 9 - d) for d in (1, 2)]

    def z_start(hops):
        for d, to, i in hops:
            hz(d, to, i).start()

    def z_recv(i):
        hz(-i, 1, i).wait_recv()


    def rc(n):
        yy = far(n)
        return remote(sibs.at[yy], sibr.at[yy], rc_s.at[n], rc_r.at[n], sibling)

    def rx(n, i):
        yy, s = far(n), side(n)
        e, to = ((2, s), (-s, -s), (s, s))[i]
        j = n * 4 + i
        return remote(xs.at[yy, rem(x + e, NX)], xr.at[yy, i], rx_s.at[j], rx_r.at[j], xpeer(to))

    def ry(n):
        yy = far(n)
        d = rem(yy - y, NY)
        return remote(ys.at[yy], yr.at[d], ry_s.at[d], ry_r.at[d], dev(yy, x, c))

    def ryf(d):
        return remote(ys.at[y], yr.at[d], ry_s.at[d], ry_r.at[d], ypeer(d))

    def project(n):
        w_copy(n).wait()
        yy = far(n)
        p = dot(w_v[yy, 0], hm[0], 0, 0) + dot(w_v[yy, 1], hm[1], 0, 0)
        part[yy] = p.reshape(4, 2, 96, 128)
        sibs[yy] = part[yy, :, 1 - c].astype(BF16)

    def project_send(n):
        project(n)
        rc(n).start()

    def chip_sum(n):
        yy = far(n)
        rc(n).wait_recv()
        total = part[yy, :, c] + sibr[yy].astype(F32)
        part[yy, :, c] = total
        xs[yy] = total.astype(BF16)
        rx(n, 0).start()
        rx(n, 1).start()

    def x_relay(n):
        yy = far(n)
        e = rem(x + side(n), NX)
        rx(n, 0).wait_recv()
        xs[yy, e] = (part[yy, e, c] + xr[yy, 0].astype(F32)).astype(BF16)
        rx(n, 2).start()

    def x_sum(n):
        yy = far(n)
        rx(n, 1).wait_recv()
        rx(n, 2).wait_recv()
        total = part[yy, x, c] + xr[yy, 1].astype(F32) + xr[yy, 2].astype(F32)

        @pl.when(n < 7)
        def _():
            ys[yy] = total.astype(BF16)
            ry(n).start()

        @pl.when(n == 7)
        def _():
            part[yy, x, c] = total

    def grad_hidden(m):
        rows.c_copy(m, 1 - c).wait_recv()
        yy = rem(y - near(m), NY)
        g = full[yy].reshape(768, 128)
        for k in range(2):
            back[k] += dot(w_v[yy, k], g, 1, 0)

    def plane_start(m):
        for s in range(3):

            @pl.when(jnp.logical_not(is_self(unit_source(s))))
            def _():
                blk = gath.at[my_q, s, my_xo // 2, my_b, my_xo % 2, c]
                remote(blk, blk, p_s.at[0], p_r.at[s], sibling).wait_recv()

        for d in (1, 7, 2, 6, 3, 5, 4):
            plane.y_send(d).start()

    def z_relay(m):
        z_recv(3)
        z_recv(9)
        z_start(relays)

    def z_finish(q):
        for s in range(3):
            d = (3 * q + s + 11) % 12
            if d not in (0, 3, 9):
                z_recv(12 - d)
            block = hbuf[rem(z + d, NZ)].astype(F32)
            mask = block[176:177]
            for k in range(2):
                hcat[q, k, :, 128 * s : 128 * s + 128] = jnp.where(
                    mask == float(k), block[:168], 0.0
                ).astype(BF16)

    def grad_weights(m):
        plane.c_copy(m, 1 - c).wait_recv()
        q, b = row_of(z, rem(y - near(m), NY))
        g = [gath[q, s, :, b].reshape(256, 128) for s in range(3)]
        g = jnp.concatenate(g, axis=1)
        for k in range(2):
            gwt[k, b] += dot(hcat[q, k], g, 1, 1)

    inputs[3].wait()
    pl.semaphore_wait(bar, greeted)

    for t in range(3):
        own = is_self(unit_dest(t))

        @pl.when(jnp.logical_not(own))
        def _():
            p_copy(t).start()

        @pl.when(own)
        def _():
            unit_slot(t)[0][...] = full[y, x, c, pl.ds(32 * t, 32), :]

    rows.start()

    for copy in inputs[:3]:
        copy.wait()

    order = jnp.broadcast_to(order_v[...].astype(F32), (128, 128)).T
    lane = lax.broadcasted_iota(jnp.int32, (128, 128), 1).astype(F32)
    pos = lax.broadcasted_iota(jnp.int32, (128, 128), 0)
    expert = (pos >= counts_v[0:1, 0:1]).astype(F32)
    routed = jnp.sum(jnp.where(order == lane, expert, 0.0), axis=0, keepdims=True)
    h = h_v[...].astype(F32)
    hbuf[z] = jnp.concatenate(
        [h, jnp.zeros((8, 128), F32), jnp.broadcast_to(routed, (16, 128))], axis=0
    ).astype(BF16)
    for k in range(2):
        hm[k] = jnp.where(routed == float(k), h, 0.0).astype(BF16)
        back[k] = jnp.zeros((168, 128), F32)
        gwt[k] = jnp.zeros((2, 168, 256), F32)

    z_start(direct)

    order = [
        (project_send, 0), (project_send, 1), (project_send, 2), (chip_sum, 0), (project_send, 3),
        (chip_sum, 1), (chip_sum, 2), (rows.level, 0), (project_send, 4), (chip_sum, 3),
        (x_relay, 0), (project_send, 5), (x_relay, 1), (chip_sum, 4), (x_relay, 2),
        (project_send, 6), (plane_start, 0), (plane.forward, 0), (chip_sum, 5), (x_relay, 3),
        (x_sum, 0), (x_sum, 1), (rows.level, 1), (x_relay, 4), (project_send, 7), (chip_sum, 6),
        (plane.forward, 1), (plane.forward, 2), (x_sum, 2), (grad_hidden, 0), (x_relay, 5),
        (z_relay, 0), (chip_sum, 7), (plane.finish, 0), (x_sum, 3), (x_sum, 4),
        (plane.forward, 3), (plane.forward, 4), (z_finish, 0), (x_relay, 6), (grad_hidden, 1),
        (grad_hidden, 2), (plane.finish, 1), (plane.forward, 5), (plane.forward, 6),
        (z_finish, 1), (x_sum, 5), (plane.finish, 2), (x_relay, 7), (z_finish, 3),
        (plane.forward, 7), (plane.finish, 3), (x_sum, 6), (plane.finish, 4), (rows.level, 2),
        (plane.finish, 5), (x_sum, 7), (grad_hidden, 3), (plane.finish, 6), (grad_hidden, 4),
        (z_finish, 2), (plane.finish, 7), (grad_weights, 0), (rows.level, 3), (grad_weights, 1),
        (grad_weights, 2), (grad_weights, 3), (grad_weights, 4), (grad_weights, 5),
        (grad_weights, 6), (rows.level, 4), (grad_weights, 7), (grad_hidden, 5), (grad_hidden, 6),
        (grad_hidden, 7),
    ]
    for stage, index in order:
        stage(index)

    gh_ref[...] = jnp.where(routed == 0.0, back[0], back[1]).astype(BF16)

    total = part[y, x, c]
    for d in range(1, NY):
        ryf(d).wait_recv()
        total = total + yr[d].astype(F32)
    out_ref[...] = total.astype(BF16)

    for k in range(2):
        for b in range(2):
            for i in range(2):
                cols = slice(256 * i + 128 * b, 256 * i + 128 * b + 128)
                gw_ref[k, :, cols] = gwt[k, b, :, 128 * i : 128 * i + 128].astype(BF16)

    for t in range(3):

        @pl.when(jnp.logical_not(is_self(unit_dest(t))))
        def _():
            p_copy(t).wait_send()

    for d in range(1, NY):
        plane.y_send(d).wait_send()
        ryf(d).wait_send()
    for d, to, i in direct + relays:
        hz(d, to, i).wait_send()

    rows.drain()

    def drain(m, carry):
        rc(m).wait_send()
        plane.drain(m)
        for i in range(3):
            rx(m, i).wait_send()
        return carry

    lax.fori_loop(0, 8, drain, 0)


def write_out(*refs):
    for i in range(3):
        refs[3 + i][...] = refs[i][...]


def shards(hidden_t, weights, grad_out_t, counts, row_order):
    vmem = pl.BlockSpec(memory_space=pltpu.VMEM)
    dma = pltpu.SemaphoreType.DMA
    blocks = (8, 4, 96, 128)
    shapes = (
        jax.ShapeDtypeStruct((96, 128), BF16),
        jax.ShapeDtypeStruct((168, 128), BF16),
        jax.ShapeDtypeStruct((2, 168, 512), BF16),
    )
    results = pl.pallas_call(
        kernel,
        out_shape=shapes,
        in_specs=[pl.BlockSpec(memory_space=pltpu.HBM)] * 5,
        out_specs=(vmem, vmem, vmem),
        scratch_shapes=[
            pltpu.VMEM((8, 2, 168, 768), BF16),
            pltpu.VMEM((8, 4, 2, 96, 128), BF16),
            pltpu.VMEM((4, 3, 2, 2, 2, 2, 32, 128), BF16),
            pltpu.VMEM((12, 192, 128), BF16),
            pltpu.VMEM((168, 128), BF16),
            pltpu.VMEM((2, 168, 128), BF16),
            pltpu.VMEM((8, 4, 2, 96, 128), F32),
            pltpu.VMEM(blocks, BF16),
            pltpu.VMEM(blocks, BF16),
            pltpu.VMEM(blocks, BF16),
            pltpu.VMEM(blocks, BF16),
            pltpu.VMEM((8, 96, 128), BF16),
            pltpu.VMEM((8, 96, 128), BF16),
            pltpu.VMEM((2, 168, 128), F32),
            pltpu.VMEM((4, 2, 168, 384), BF16),
            pltpu.VMEM((2, 2, 168, 256), F32),
            pltpu.VMEM((1, 2), jnp.int32),
            pltpu.VMEM((1, 128), jnp.int32),
            dma((8,)), dma((4,)), dma((3,)), dma((3,)), dma((12,)), dma((12,)),
            dma((8, 2)), dma((8, 2)), dma((4,)), dma((4,)), dma((8,)), dma((8,)),
            dma((8,)), dma((8,)), dma((32,)), dma((32,)), dma((8,)), dma((8,)),
            dma((8,)), dma((8,)), dma((32,)), dma((32,)), dma((8,)), dma((8,)),
        ],
        compiler_params=pltpu.CompilerParams(
            collective_id=0, has_side_effects=True, vmem_limit_bytes=60 << 20
        ),
        name="moe_down",
    )(hidden_t, weights, grad_out_t, counts, row_order)
    return pl.pallas_call(
        write_out,
        out_shape=shapes,
        in_specs=[vmem] * 3,
        out_specs=(vmem,) * 3,
        name="write_out",
    )(*results)


def solution(mesh):
    in_specs = (P("et", "dp"), P(None, "et", None), P("et", "dp"), P("dp", None), P("dp", None))
    out_specs = (P("et", "dp"), P("et", "dp"), P(None, "et", "dp"))
    return jax.shard_map(shards, mesh=mesh, in_specs=in_specs, out_specs=out_specs, check_vma=False)
```

```python
import jax
import jax.numpy as jnp
from jax import lax
from jax.experimental import pallas as pl
from jax.experimental.pallas import tpu as pltpu
from jax.sharding import PartitionSpec as P

MESH = pl.DeviceIdType.MESH
NY, NX, NZ = 8, 4, 12
BF16, F32 = jnp.bfloat16, jnp.float32


def dot(a, b, ca, cb):
    return lax.dot_general(a, b, (((ca,), (cb,)), ((), ())), preferred_element_type=F32)


def kernel(
    h_hbm, w_hbm, g_hbm, counts_hbm, order_hbm, out_ref, gh_ref, gw_ref,
    w_v, full, gath, hbuf, h_v, hm, part, sibs, sibr, xs, xr, ys, yr, back, hcat, gwt, counts_v, order_v,
    wsem, in_sem, p_s, p_r, hz_s, hz_r,
    a1y_s, a1y_r, a1x_s, a1x_r, a1c_s, a1c_r,
    a2y_s, a2y_r, a2x_s, a2x_r, a2c_s, a2c_r,
    rc_s, rc_r, rx_s, rx_r, ry_s, ry_r,
):
    z = lax.axis_index("dp")
    et = lax.axis_index("et")
    y, x, c = et // 8, (et // 2) % 4, et % 2

    def dev(yy, xx, cc):
        return (z, (yy * 4 + xx) * 2 + cc)

    def rem(a, n):
        return lax.rem(a + n, n)

    def ypeer(d):
        return dev(rem(y + d, NY), x, c)

    def xpeer(e):
        return dev(y, rem(x + e, NX), c)

    def zpeer(d):
        return (rem(z + d, NZ), et)

    sibling = dev(y, x, 1 - c)

    def remote(src, dst, ss, rs, peer):
        return pltpu.make_async_remote_copy(
            src_ref=src, dst_ref=dst, send_sem=ss, recv_sem=rs, device_id=peer, device_id_type=MESH
        )

    def corner(i):
        chip = i * 16 // 6
        return chip // 4, rem(chip % 4 - jnp.where(i % 3 == 0, 1, 0), NX)

    def groups_of(k, i):
        rel = rem(k - i, NZ) + 1
        return (rel // 3) % 4, rel % 3

    def group(i, q, s):
        return (i + 3 * q + s + 11) % NZ

    def place(i, w, q):
        yc, xc = corner(i)
        xo, b, cc = w // 8 * 2 + w // 2 % 2, w // 4 % 2, w % 2
        rank = jnp.where(q == 0, 3, jnp.where(q == 3, 2, 2 - q))
        yy = (yc + jnp.where(b == 1, 1 + rank, 8 - rank)) % NY
        return (yy * 4 + (xc + xo) % NX) * 2 + cc

    def row_of(i, yy):
        dy = rem(yy - corner(i)[0], NY)
        b = (dy + 3) % 8 // 4
        rank = jnp.where(b == 1, dy - 1, (8 - dy) % 8)
        return jnp.where(rank == 3, 0, jnp.where(rank == 2, 3, 2 - rank)), b

    def col_of(i, xx):
        return rem(xx - corner(i)[1], NX)

    def unit(t):
        u = et * 3 + t
        return u // 16, u % 16

    def unit_dest(t):
        i, w = unit(t)
        return i, place(i, w, groups_of(z, i)[0])

    def unit_slot(t):
        i, w = unit(t)
        q, s = groups_of(z, i)
        return gath.at[q, s, w // 8, w // 4 % 2, w // 2 % 2, w % 2], s

    my_q, my_b = row_of(z, y)
    my_xo = col_of(z, x)
    my_w = my_xo // 2 * 8 + my_b * 4 + my_xo % 2 * 2 + c

    def unit_source(s):
        return group(z, my_q, s), (z * 16 + my_w) // 3

    def far(n):
        return rem(y + 4 + (1 - 2 * (n % 2)) * ((n + 1) // 2), NY)

    def near(m):
        return ((m + 1) // 2) * (1 - 2 * ((m + 1) % 2))

    def side(m):
        return 1 - 2 * (m % 2)

    inputs = [
        pltpu.make_async_copy(src, dst, in_sem.at[i])
        for i, (src, dst) in enumerate(
            [
                (order_hbm, order_v),
                (counts_hbm, counts_v),
                (h_hbm, h_v),
                (g_hbm, full.at[y, x, c]),
            ]
        )
    ]
    for copy in inputs[::-1]:
        copy.start()

    def w_copy(n):
        yy = far(n)
        cols = pl.ds(pl.multiple_of(yy * 768, 768), 768)
        return pltpu.make_async_copy(w_hbm.at[:, :, cols], w_v.at[yy], wsem.at[n])

    for n in range(8):
        w_copy(n).start()

    bar = pltpu.get_barrier_semaphore()

    def greet(peer):
        pl.semaphore_signal(bar, inc=1, device_id=peer, device_id_type=MESH)

    def is_self(peer):
        return jnp.logical_and(peer[0] == z, peer[1] == et)

    greeted = 7 + 3 + 1 + 6
    for t in range(3):
        for peer in (unit_dest(t), unit_source(t)):
            own = is_self(peer)
            greeted = greeted + jnp.where(own, 0, 1)

            @pl.when(jnp.logical_not(own))
            def _():
                greet(peer)

    for d in (4, 3, 5, 2, 6, 1, 7):
        greet(ypeer(d))
    for d in (3, -3, 2, -2, 1, -1):
        greet(zpeer(d))
    for e in (1, 2, 3):
        greet(xpeer(e))
    greet(sibling)

    def p_copy(t):
        dst, s = unit_slot(t)
        src = full.at[y, x, c, pl.ds(32 * t, 32)]
        return remote(src, dst, p_s.at[t], p_r.at[s], unit_dest(t))

    class Gather:
        def __init__(self, block, pair, sems):
            self.block, self.pair = block, pair
            self.ys, self.yr, self.xs, self.xr, self.cs, self.cr = sems

        def at(self, m, e):
            return self.block(rem(y - near(m), NY), rem(x + e, NX))

        def y_send(self, d):
            blk = self.block(y, x)
            return remote(blk, blk, self.ys.at[d], self.yr.at[d], ypeer(d))

        def y_recv(self, m):
            d = rem(near(m), NY)
            blk = self.at(m, 0)
            remote(blk, blk, self.ys.at[d], self.yr.at[d], ypeer(d)).wait_recv()

        def x_copy(self, m, e, i, to):
            blk = self.at(m, e)
            return remote(blk, blk, self.xs.at[m * 4 + i], self.xr.at[m * 4 + i], xpeer(to))

        def forward(self, m):
            @pl.when(m > 0)
            def _():
                self.y_recv(m)

            self.x_copy(m, 0, 0, 1).start()
            self.x_copy(m, 0, 1, -1).start()
            self.x_copy(m, 0, 2, 2).start()

        def finish(self, m):
            self.x_copy(m, -1, 0, 1).wait_recv()
            self.x_copy(m, 1, 1, -1).wait_recv()
            self.x_copy(m, 2, 2, 2).wait_recv()
            self.c_copy(m, c).start()

        def c_copy(self, m, cc):
            blk = self.pair(rem(y - near(m), NY), cc)
            return remote(blk, blk, self.cs.at[m], self.cr.at[m], sibling)

        def drain(self, m):
            self.x_copy(m, 0, 0, 1).wait_send()
            self.x_copy(m, 0, 1, -1).wait_send()
            self.x_copy(m, 0, 2, 2).wait_send()
            self.c_copy(m, c).wait_send()

    class Ring:
        def x_copy(self, e, e_from):
            blk = full.at[y, rem(x - e_from, NX), c]
            return remote(blk, blk, a1x_s.at[e], a1x_r.at[e], xpeer(e))

        def y_copy(self, way, s, g, shift):
            yy = rem(y - way * (s + shift), NY)
            blk = full.at[yy, pl.ds(2 * g, 2), c]
            i = (4 if way < 0 else 0) + s
            return remote(blk, blk, a1y_s.at[i, g], a1y_r.at[i, g], ypeer(way))

        def c_copy(self, m, cc):
            blk = full.at[rem(y - near(m), NY), :, cc]
            return remote(blk, blk, a1c_s.at[m], a1c_r.at[m], sibling)

        def hops(self, s):
            return [(w, g) for g in range(2) for w in (1, -1) if s < 3 or (w > 0) == (g == 0)]

        def start(self):
            for e in (1, 3, 2):
                self.x_copy(e, 0).start()

        def level(self, s):
            if s == 0:
                for e in (1, 3, 2):
                    self.x_copy(e, e).wait_recv()
            if s < 4:
                for w, g in self.hops(s):
                    if s > 0:
                        self.y_copy(w, s - 1, g, 1).wait_recv()
                    self.y_copy(w, s, g, 0).start()
                if s == 3:
                    for w, g in self.hops(0):
                        if (w, g) not in self.hops(3):
                            self.y_copy(w, 2, g, 1).wait_recv()
            else:
                for w, g in self.hops(3):
                    self.y_copy(w, 3, g, 1).wait_recv()
            for m in {0: (0,), 4: (7,)}.get(s, (2 * s - 1, 2 * s)):
                self.c_copy(m, c).start()

        def drain(self):
            for e in (1, 3, 2):
                self.x_copy(e, 0).wait_send()
            for s in range(4):
                for w, g in self.hops(s):
                    self.y_copy(w, s, g, 0).wait_send()
            for m in range(8):
                self.c_copy(m, c).wait_send()

    rows = Ring()
    def plane_block(yy, xx):
        q, b = row_of(z, yy)
        xo = col_of(z, xx)
        return gath.at[q, :, xo // 2, b, xo % 2, c]

    def plane_pair(yy, cc):
        q, b = row_of(z, yy)
        return gath.at[q, :, :, b, :, cc]

    plane = Gather(
        plane_block,
        plane_pair,
        (a2y_s, a2y_r, a2x_s, a2x_r, a2c_s, a2c_r),
    )


    def hz(d, to, i):
        k = rem(z + d, NZ)
        return remote(hbuf.at[k], hbuf.at[k], hz_s.at[i], hz_r.at[i], zpeer(to))

    direct = [(0, d, d % 12) for d in (3, -3, 2, -2, 1, -1)]
    relays = [(-3, d, d + 3) for d in (1, 2, 3)] + [(3, -d, 9 - d) for d in (1, 2)]

    def z_start(hops):
        for d, to, i in hops:
            hz(d, to, i).start()

    def z_recv(i):
        hz(-i, 1, i).wait_recv()


    def rc(n):
        yy = far(n)
        return remote(sibs.at[yy], sibr.at[yy], rc_s.at[n], rc_r.at[n], sibling)

    def rx(n, i):
        yy, s = far(n), side(n)
        e, to = ((2, s), (-s, -s), (s, s))[i]
        j = n * 4 + i
        return remote(xs.at[yy, rem(x + e, NX)], xr.at[yy, i], rx_s.at[j], rx_r.at[j], xpeer(to))

    def ry(n):
        yy = far(n)
        d = rem(yy - y, NY)
        return remote(ys.at[yy], yr.at[d], ry_s.at[d], ry_r.at[d], dev(yy, x, c))

    def ryf(d):
        return remote(ys.at[y], yr.at[d], ry_s.at[d], ry_r.at[d], ypeer(d))

    def project(n):
        w_copy(n).wait()
        yy = far(n)
        p = dot(w_v[yy, 0], hm[0], 0, 0) + dot(w_v[yy, 1], hm[1], 0, 0)
        part[yy] = p.reshape(4, 2, 96, 128)
        sibs[yy] = part[yy, :, 1 - c].astype(BF16)

    def project_send(n):
        project(n)
        rc(n).start()

    def chip_sum(n):
        yy = far(n)
        rc(n).wait_recv()
        total = part[yy, :, c] + sibr[yy].astype(F32)
        part[yy, :, c] = total
        xs[yy] = total.astype(BF16)
        rx(n, 0).start()
        rx(n, 1).start()

    def x_relay(n):
        yy = far(n)
        e = rem(x + side(n), NX)
        rx(n, 0).wait_recv()
        xs[yy, e] = (part[yy, e, c] + xr[yy, 0].astype(F32)).astype(BF16)
        rx(n, 2).start()

    def x_sum(n):
        yy = far(n)
        rx(n, 1).wait_recv()
        rx(n, 2).wait_recv()
        total = part[yy, x, c] + xr[yy, 1].astype(F32) + xr[yy, 2].astype(F32)

        @pl.when(n < 7)
        def _():
            ys[yy] = total.astype(BF16)
            ry(n).start()

        @pl.when(n == 7)
        def _():
            part[yy, x, c] = total

    def grad_hidden(m):
        rows.c_copy(m, 1 - c).wait_recv()
        yy = rem(y - near(m), NY)
        g = full[yy].reshape(768, 128)
        for k in range(2):
            back[k] += dot(w_v[yy, k], g, 1, 0)

    def plane_start(m):
        for s in range(3):

            @pl.when(jnp.logical_not(is_self(unit_source(s))))
            def _():
                blk = gath.at[my_q, s, my_xo // 2, my_b, my_xo % 2, c]
                remote(blk, blk, p_s.at[0], p_r.at[s], sibling).wait_recv()

        for d in (1, 7, 2, 6, 3, 5, 4):
            plane.y_send(d).start()

    def z_relay(m):
        z_recv(3)
        z_recv(9)
        z_start(relays)

    def z_finish(q):
        for s in range(3):
            d = (3 * q + s + 11) % 12
            if d not in (0, 3, 9):
                z_recv(12 - d)
            block = hbuf[rem(z + d, NZ)].astype(F32)
            mask = block[176:177]
            for k in range(2):
                hcat[q, k, :, 128 * s : 128 * s + 128] = jnp.where(
                    mask == float(k), block[:168], 0.0
                ).astype(BF16)

    def grad_weights(m):
        plane.c_copy(m, 1 - c).wait_recv()
        q, b = row_of(z, rem(y - near(m), NY))
        g = [gath[q, s, :, b].reshape(256, 128) for s in range(3)]
        g = jnp.concatenate(g, axis=1)
        for k in range(2):
            gwt[k, b] += dot(hcat[q, k], g, 1, 1)

    inputs[3].wait()
    pl.semaphore_wait(bar, greeted)

    for t in range(3):
        own = is_self(unit_dest(t))

        @pl.when(jnp.logical_not(own))
        def _():
            p_copy(t).start()

        @pl.when(own)
        def _():
            unit_slot(t)[0][...] = full[y, x, c, pl.ds(32 * t, 32), :]

    rows.start()

    for copy in inputs[:3]:
        copy.wait()

    order = jnp.broadcast_to(order_v[...].astype(F32), (128, 128)).T
    lane = lax.broadcasted_iota(jnp.int32, (128, 128), 1).astype(F32)
    pos = lax.broadcasted_iota(jnp.int32, (128, 128), 0)
    expert = (pos >= counts_v[0:1, 0:1]).astype(F32)
    routed = jnp.sum(jnp.where(order == lane, expert, 0.0), axis=0, keepdims=True)
    h = h_v[...].astype(F32)
    hbuf[z] = jnp.concatenate(
        [h, jnp.zeros((8, 128), F32), jnp.broadcast_to(routed, (16, 128))], axis=0
    ).astype(BF16)
    for k in range(2):
        hm[k] = jnp.where(routed == float(k), h, 0.0).astype(BF16)
        back[k] = jnp.zeros((168, 128), F32)
        gwt[k] = jnp.zeros((2, 168, 256), F32)

    z_start(direct)

    order = [
        (project_send, 0), (project_send, 1), (project_send, 2), (chip_sum, 0), (project_send, 3),
        (chip_sum, 1), (chip_sum, 2), (rows.level, 0), (project_send, 4), (chip_sum, 3),
        (x_relay, 0), (project_send, 5), (plane_start, 0), (plane.forward, 0), (chip_sum, 4),
        (x_relay, 1), (x_relay, 2), (project_send, 6), (chip_sum, 5), (x_relay, 3), (x_sum, 0),
        (plane.forward, 1), (plane.forward, 2), (rows.level, 1), (project_send, 7), (chip_sum, 6),
        (plane.finish, 0), (x_relay, 4), (x_sum, 1), (x_sum, 2), (plane.forward, 3),
        (plane.forward, 4), (z_relay, 0), (x_relay, 5), (z_finish, 0), (chip_sum, 7), (x_sum, 3),
        (grad_hidden, 0), (grad_hidden, 1), (plane.forward, 5), (plane.forward, 6),
        (plane.finish, 1), (x_relay, 6), (grad_hidden, 2), (x_sum, 4), (plane.finish, 2),
        (z_finish, 1), (rows.level, 2), (plane.forward, 7), (plane.finish, 3), (z_finish, 3),
        (x_sum, 5), (plane.finish, 4), (grad_hidden, 3), (x_relay, 7), (grad_hidden, 4),
        (plane.finish, 5), (x_sum, 6), (plane.finish, 6), (rows.level, 3), (x_sum, 7),
        (plane.finish, 7), (z_finish, 2), (grad_weights, 0), (grad_weights, 1), (grad_weights, 2),
        (rows.level, 4), (grad_weights, 3), (grad_weights, 4), (grad_weights, 5),
        (grad_weights, 6), (grad_weights, 7), (grad_hidden, 5), (grad_hidden, 6),
        (grad_hidden, 7),
    ]
    for stage, index in order:
        stage(index)

    gh_ref[...] = jnp.where(routed == 0.0, back[0], back[1]).astype(BF16)

    total = part[y, x, c]
    for d in range(1, NY):
        ryf(d).wait_recv()
        total = total + yr[d].astype(F32)
    out_ref[...] = total.astype(BF16)

    for k in range(2):
        for b in range(2):
            for i in range(2):
                cols = slice(256 * i + 128 * b, 256 * i + 128 * b + 128)
                gw_ref[k, :, cols] = gwt[k, b, :, 128 * i : 128 * i + 128].astype(BF16)

    for t in range(3):

        @pl.when(jnp.logical_not(is_self(unit_dest(t))))
        def _():
            p_copy(t).wait_send()

    for d in range(1, NY):
        plane.y_send(d).wait_send()
        ryf(d).wait_send()
    for d, to, i in direct + relays:
        hz(d, to, i).wait_send()

    rows.drain()

    def drain(m, carry):
        rc(m).wait_send()
        plane.drain(m)
        for i in range(3):
            rx(m, i).wait_send()
        return carry

    lax.fori_loop(0, 8, drain, 0)


def write_out(*refs):
    for i in range(3):
        refs[3 + i][...] = refs[i][...]


def shards(hidden_t, weights, grad_out_t, counts, row_order):
    vmem = pl.BlockSpec(memory_space=pltpu.VMEM)
    dma = pltpu.SemaphoreType.DMA
    blocks = (8, 4, 96, 128)
    shapes = (
        jax.ShapeDtypeStruct((96, 128), BF16),
        jax.ShapeDtypeStruct((168, 128), BF16),
        jax.ShapeDtypeStruct((2, 168, 512), BF16),
    )
    results = pl.pallas_call(
        kernel,
        out_shape=shapes,
        in_specs=[pl.BlockSpec(memory_space=pltpu.HBM)] * 5,
        out_specs=(vmem, vmem, vmem),
        scratch_shapes=[
            pltpu.VMEM((8, 2, 168, 768), BF16),
            pltpu.VMEM((8, 4, 2, 96, 128), BF16),
            pltpu.VMEM((4, 3, 2, 2, 2, 2, 32, 128), BF16),
            pltpu.VMEM((12, 192, 128), BF16),
            pltpu.VMEM((168, 128), BF16),
            pltpu.VMEM((2, 168, 128), BF16),
            pltpu.VMEM((8, 4, 2, 96, 128), F32),
            pltpu.VMEM(blocks, BF16),
            pltpu.VMEM(blocks, BF16),
            pltpu.VMEM(blocks, BF16),
            pltpu.VMEM(blocks, BF16),
            pltpu.VMEM((8, 96, 128), BF16),
            pltpu.VMEM((8, 96, 128), BF16),
            pltpu.VMEM((2, 168, 128), F32),
            pltpu.VMEM((4, 2, 168, 384), BF16),
            pltpu.VMEM((2, 2, 168, 256), F32),
            pltpu.VMEM((1, 2), jnp.int32),
            pltpu.VMEM((1, 128), jnp.int32),
            dma((8,)), dma((4,)), dma((3,)), dma((3,)), dma((12,)), dma((12,)),
            dma((8, 2)), dma((8, 2)), dma((4,)), dma((4,)), dma((8,)), dma((8,)),
            dma((8,)), dma((8,)), dma((32,)), dma((32,)), dma((8,)), dma((8,)),
            dma((8,)), dma((8,)), dma((32,)), dma((32,)), dma((8,)), dma((8,)),
        ],
        compiler_params=pltpu.CompilerParams(
            collective_id=0, has_side_effects=True, vmem_limit_bytes=60 << 20
        ),
        name="moe_down",
    )(hidden_t, weights, grad_out_t, counts, row_order)
    return pl.pallas_call(
        write_out,
        out_shape=shapes,
        in_specs=[vmem] * 3,
        out_specs=(vmem,) * 3,
        name="write_out",
    )(*results)


def solution(mesh):
    in_specs = (P("et", "dp"), P(None, "et", None), P("et", "dp"), P("dp", None), P("dp", None))
    out_specs = (P("et", "dp"), P("et", "dp"), P(None, "et", "dp"))
    return jax.shard_map(shards, mesh=mesh, in_specs=in_specs, out_specs=out_specs, check_vma=False)
```
